32 devices in a mesh: parts: 2 (over y), group: 4 (over z), local: 4 (over x, core).
Axes of the slice: x: 2, y: 2, z: 4, core: 2. Of those that a mesh axis runs over, the one named last changes fastest.
Arguments:
- tokens: bfloat16 [4096, 3584], P(('parts', 'group', 'local')), parts along dimension 0, may hold values from -6 to 6
- routes: int32 [4096, 8], P(('parts', 'group', 'local')), parts along dimension 0, may hold values from 0 to 15, as said below
- gate_weights: bfloat16 [4096, 8], P(('parts', 'group', 'local')), parts along dimension 0, may hold values from 0.099609375 to 1
- w_expert: bfloat16 [16, 3584, 1536], P(('group', 'local')), may hold values from -0.09375 to 0.09375
Outputs:
- mixture: bfloat16 [4096, 1536], P(('parts', 'group', 'local')), parts along dimension 0
The draws below stay inside these ranges and needn't reach their ends.
There are 2 independent parts, one for each index of `parts`. The reference program is written for one: setup_inputs(seed, part) draws one part's arguments, and reference() takes and returns one part's arrays. A program takes and returns all parts, laid end to end along the dimension named above; an argument that names none is the same for every part. Nothing has to cross between parts.
Inputs may be any that keep to these rules, and one draw needn't show every extreme that they name: `routes`: A row names 8 different experts lying in 4 node groups (expert e lies in group e // 4), two in each; the rows of one device name every expert exactly 64 times, and so each node group in exactly 128 rows.
All inputs are finite; a program needn't handle non-finite values.
Results may differ from the reference program's by a relative error of at most 0.008.
Values may be sent and summed in bfloat16 or wider, within the bound.
A program may use at most 128 MiB of HBM per device.

```python
import math
import jax
import jax.numpy as jnp
from jax import lax

D = 3584
FF = 1536
TOP = 8
TOK_DEV = 128
GROUPS = 4
PER_GROUP = 4
EXPERTS = 16
CAP = 64
TOKENS = 2048


def draw_routes(key, part):
    key = jax.random.fold_in(key, 7)
    devices = GROUPS * PER_GROUP
    halves = PER_GROUP // 2

    def one_device(dev_key):
        key_tok, key_grp, key_loc, key_shift = jax.random.split(dev_key, 4)
        shuffled = jax.random.permutation(key_tok, TOK_DEV)
        offset = shuffled % GROUPS
        quotient = shuffled // GROUPS
        group_perm = jax.random.permutation(key_grp, GROUPS)
        local_perm = jax.vmap(lambda sub_key: jax.random.permutation(sub_key, PER_GROUP))(jax.random.split(key_loc, GROUPS))
        shifts = jax.random.randint(key_shift, (4,), 0, halves)
        columns = []
        for column in range(4):
            group_id = group_perm[(offset + column) % GROUPS]
            member = (quotient + shifts[column]) % halves
            for second in range(2):
                local_id = local_perm[group_id, 2 * member + second]
                columns.append(group_id * PER_GROUP + local_id)
        return jnp.stack(columns, axis=1)
    result = jax.vmap(one_device)(jax.random.split(key, devices))
    return result.reshape(TOK_DEV * devices, TOP).astype(jnp.int32)


def level_of(rng, extent, cuts, least, largest):
    def one(dim, shards_of):
        heights = jax.random.uniform(jax.random.fold_in(jax.random.fold_in(rng, 6), dim), (shards_of,), jnp.float32, least / len(cuts), largest / len(cuts))
        return jnp.repeat(jnp.exp(heights), extent[dim] // shards_of).reshape((-1,) + (1,) * (len(extent) - dim - 1))

    gain = one(*cuts[0])
    for cut in cuts[1:]:
        gain = gain * one(*cut)
    return gain


def centred(stream_key, shape, scale, most, cuts=(), kind=jnp.bfloat16):
    gain = level_of(stream_key, shape, cuts, -0.22, 0.18) if cuts else 1.0
    array = jax.random.normal(stream_key, shape, jnp.float32) * scale * gain
    return jnp.minimum(jnp.maximum(array, -most), most).astype(kind)


def setup_inputs(seed: int = 0, part: int = 0) -> dict:
    splits = jax.random.split(jax.random.key(seed), 5)
    own_keys = jax.random.split(jax.random.fold_in(splits[4], part), 5)
    return {
        "tokens": centred(own_keys[0], (TOKENS, D), 1.0, 6.0, ((0, 16),)),
        "routes": draw_routes(jax.random.fold_in(jax.random.fold_in(splits[4], part), 71), part),
        "gate_weights": jnp.clip(jnp.exp(math.log(1.0) - 2.306499 * jax.random.uniform(own_keys[2], (TOKENS, TOP), jnp.float32) ** level_of(own_keys[2], (TOKENS, TOP), ((0, 16),), -0.2, 0.2)), 0.099609375, 1.0).astype(jnp.bfloat16),
        "w_expert": centred(splits[3], (EXPERTS, D, FF), D ** -0.5, 0.09375, ((0, 16),)),
    }


def reference(tokens, routes, gate_weights, w_expert):
    devices = GROUPS * PER_GROUP
    pairs = TOK_DEV * TOP
    flat_ids = routes.reshape(devices, pairs)
    by_expert = jnp.argsort(flat_ids, axis=1, stable=True).astype(jnp.int32)
    offsets = (jnp.arange(devices, dtype=jnp.int32) * TOK_DEV)[:, None]
    token_of = by_expert // TOP + offsets
    token_of = token_of.reshape(devices, EXPERTS, CAP).transpose(1, 0, 2).reshape(EXPERTS, devices * CAP)

    def apply_expert(packed):
        index, weight = packed
        slot_rows = tokens[index]
        return jax.nn.silu(jnp.dot(slot_rows, weight, preferred_element_type=jnp.float32)).astype(jnp.bfloat16)

    outputs = lax.map(apply_expert, (token_of, w_expert))
    outputs = outputs.reshape(EXPERTS, devices, CAP, FF).transpose(1, 0, 2, 3).reshape(devices, EXPERTS * CAP, FF)
    inverse = jnp.argsort(by_expert, axis=1).astype(jnp.int32)
    pair_out = jnp.take_along_axis(outputs, inverse[:, :, None], axis=1)
    pair_out = pair_out.reshape(TOKENS, TOP, FF)
    group_of = routes // PER_GROUP
    pick_ids = jnp.arange(TOP, dtype=jnp.int32)
    same = group_of[:, :, None] == group_of[:, None, :]
    others = same & (pick_ids[:, None] != pick_ids[None, :])[None, :, :]
    partner = jnp.sum(jnp.where(others, pick_ids[None, None, :], 0), axis=2).astype(jnp.int32)
    earlier = jnp.sum(jnp.where(same & (pick_ids[None, :] < pick_ids[:, None])[None, :, :], 1, 0), axis=2)
    weighted = gate_weights.astype(jnp.float32)[:, :, None] * pair_out.astype(jnp.float32)
    group_sum = (weighted + jnp.take_along_axis(weighted, partner[:, :, None], axis=1)).astype(jnp.bfloat16)
    mixture = jnp.sum(jnp.where((earlier == 0)[:, :, None], group_sum.astype(jnp.float32), jnp.float32(0.0)), axis=1)
    return mixture.astype(jnp.bfloat16)
```

```python
import functools

import jax
import jax.numpy as jnp
from jax import lax
from jax.experimental import pallas as pl
from jax.experimental.pallas import tpu as pltpu
from jax.sharding import PartitionSpec as P

SPEC = P(("parts", "group", "local"), None)


def routed(tokens, routes, gate_weights, w_expert):
    tok_rows, picks = routes.shape
    groups = lax.axis_size("group")
    per_group = lax.axis_size("local")
    experts = groups * per_group
    capacity = tok_rows * picks // experts
    weight = w_expert[0]
    gates = gate_weights.astype(jnp.float32)
    group_of = routes // per_group
    pick_ids = jnp.arange(picks, dtype=jnp.int32)
    same = group_of[:, :, None] == group_of[:, None, :]
    others = same & (pick_ids[:, None] != pick_ids[None, :])[None, :, :]
    partner = jnp.sum(jnp.where(others, pick_ids[None, None, :], 0), axis=2)
    earlier = jnp.sum(
        jnp.where(same & (pick_ids[None, :] < pick_ids[:, None])[None, :, :], 1, 0), axis=2
    ).astype(jnp.int32)
    first = (earlier == 0)[:, :, None]
    flat_ids = routes.reshape(-1)
    onehot = (flat_ids[:, None] == jnp.arange(experts, dtype=jnp.int32)[None, :]).astype(jnp.int32)
    before = jnp.cumsum(onehot, axis=0) - onehot
    slot_of = flat_ids * capacity + jnp.sum(before * onehot, axis=1)
    pair_tokens = jnp.arange(tok_rows * picks, dtype=jnp.int32) // picks
    source = jnp.zeros((experts * capacity,), jnp.int32).at[slot_of].set(pair_tokens)
    outgoing = tokens[source]
    arrived = lax.all_to_all(
        outgoing.reshape(experts, capacity, -1),
        ("group", "local"),
        split_axis=0,
        concat_axis=0,
        tiled=True,
    )
    flatrows = arrived.reshape(-1, arrived.shape[-1])
    result = (
        jax.nn.silu(jnp.dot(flatrows, weight, preferred_element_type=jnp.float32))
        .astype(jnp.bfloat16)
        .reshape(experts, capacity, -1)
    )
    returned = lax.all_to_all(result, ("group", "local"), split_axis=0, concat_axis=0, tiled=True)
    pair_out = returned.reshape(experts * capacity, -1)[slot_of].reshape(tok_rows, picks, -1)
    weighted = gates[:, :, None] * pair_out.astype(jnp.float32)
    group_sum = (weighted + jnp.take_along_axis(weighted, partner[:, :, None], axis=1)).astype(
        jnp.bfloat16
    )
    return jnp.sum(
        jnp.where(first, group_sum.astype(jnp.float32), jnp.float32(0.0)), axis=1
    ).astype(jnp.bfloat16)


def tile_of(width, most):
    tile = most
    while width % tile:
        tile -= 128
    return tile


def fused_kernel(
    G, L, cap,
    tok_ref, meta_ref, w_ref, out_ref,
    w, tok, meta, pick, comb, sel, rows, outs, res, gsum, gin,
    load_sem, meta_s, meta_r, up_s, down_s, tok_r, row_s, row_r, res_s, res_r, gs_s, gs_r,
):
    T, D = tok_ref.shape
    FF = w_ref.shape[1]
    picks = meta_ref.shape[0] // 2
    g = lax.axis_index("group")
    l = lax.axis_index("local")

    low = jnp.minimum(g, G - 1 - g)
    side = jnp.where(g < G - 1 - g, 1, -1)

    def origin(i):
        near = (i + 1) // 2 * jnp.where(i % 2 == 1, -1, 1)
        return g + jnp.where(i <= 2 * low, near, (i - low) * side)

    def far(k):
        return lax.rem(g + k, G)

    def peer(k):
        return lax.rem(l + k, L)

    def remote(src, dst, send, recv, group=None, local=None):
        where = {}
        if group is not None:
            where["group"] = group
        if local is not None:
            where["local"] = local
        return pltpu.make_async_remote_copy(
            src_ref=src, dst_ref=dst, send_sem=send, recv_sem=recv,
            device_id=where, device_id_type=pl.DeviceIdType.MESH,
        )

    def meta_copy(k):
        return remote(meta.at[g], meta.at[g], meta_s.at[k], meta_r.at[g], group=far(k))

    def up_copy(o):
        return remote(tok.at[o], tok.at[o], up_s.at[o], tok_r.at[o], group=g + 1)

    def down_copy(o):
        return remote(tok.at[o], tok.at[o], down_s.at[o], tok_r.at[o], group=g - 1)

    def row_copy(o, k):
        e = peer(k)
        return remote(sel.at[o, e], rows.at[o, l], row_s.at[o, e], row_r.at[o, l], local=e)

    def res_copy(o, k):
        e = peer(k)
        return remote(outs.at[o, e], res.at[o, l], res_s.at[o, e], res_r.at[o, l], local=e)

    def gs_copy(o):
        return remote(gsum.at[o], gin.at[g], gs_s.at[o], gs_r.at[g], group=o)

    load_meta = pltpu.make_async_copy(meta_ref, meta.at[g], load_sem.at[0])
    load_tok = pltpu.make_async_copy(tok_ref, tok.at[g], load_sem.at[1])
    load_w = pltpu.make_async_copy(w_ref, w, load_sem.at[2])
    load_meta.start()
    load_tok.start()
    load_w.start()

    barrier = pltpu.get_barrier_semaphore()
    for k in range(1, G):
        pl.semaphore_signal(
            barrier, inc=1, device_id={"group": far(k)}, device_id_type=pl.DeviceIdType.MESH
        )
    for k in range(1, L):
        pl.semaphore_signal(
            barrier, inc=1, device_id={"local": peer(k)}, device_id_type=pl.DeviceIdType.MESH
        )
    pl.semaphore_wait(barrier, G + L - 2)

    load_meta.wait()
    for k in range(1, G):
        meta_copy(k).start()
    load_tok.wait()

    def arrive(i):
        o = origin(i)

        @pl.when(o != g)
        def _():
            pltpu.make_async_copy(tok.at[o], tok.at[o], tok_r.at[o]).wait()

        @pl.when((o <= g) & (g < G - 1))
        def _():
            up_copy(o).start()

        @pl.when((o >= g) & (g > 0))
        def _():
            down_copy(o).start()

        @pl.when(o != g)
        def _():
            pltpu.make_async_copy(meta.at[o], meta.at[o], meta_r.at[o]).wait()

        chosen = meta[o, 0:picks, :]
        gates = meta[o, picks : 2 * picks, :]
        line = lax.broadcasted_iota(jnp.int32, (picks, T), 0)
        members = jnp.zeros((picks, T), jnp.float32)
        mine, scale = [], []
        for e in range(L):
            hit = chosen == (g * L + e).astype(jnp.float32)
            mine.append(jnp.sum(jnp.where(hit, 1.0, 0.0), axis=0, keepdims=True))
            scale.append(jnp.sum(jnp.where(hit, gates, 0.0), axis=0, keepdims=True))
            members = members + jnp.where(line == e, mine[e], 0.0)
        ahead = jnp.where(
            lax.broadcasted_iota(jnp.int32, (T, T), 0) < lax.broadcasted_iota(jnp.int32, (T, T), 1),
            1.0, 0.0,
        )
        rank = jnp.dot(members, ahead, preferred_element_type=jnp.float32)
        slot = lax.broadcasted_iota(jnp.int32, (cap, T), 0).astype(jnp.float32)
        for e in range(L):
            here = jnp.where((slot == rank[e : e + 1, :]) & (mine[e] > 0.5), 1.0, 0.0)
            pick[o, e * cap : (e + 1) * cap, :] = here.astype(jnp.bfloat16)
            comb[o, e * cap : (e + 1) * cap, :] = here * scale[e]

        tile = tile_of(D, 512)

        def part(n, carry):
            at = pl.ds(pl.multiple_of(n * tile, tile), tile)
            got = jnp.dot(pick[o], tok[o, :, at], preferred_element_type=jnp.float32)
            sel[o, :, :, at] = got.astype(jnp.bfloat16).reshape(L, cap, tile)
            return carry

        lax.fori_loop(0, D // tile, part, 0)
        for k in range(1, L):
            row_copy(o, k).start()
        keep = pltpu.make_async_copy(sel.at[o, l], rows.at[o, l], row_r.at[o, l])
        keep.start()

    def expert(i):
        o = origin(i)
        for k in range(L):
            e = peer(k)
            pltpu.make_async_copy(rows.at[o, e], rows.at[o, e], row_r.at[o, e]).wait()
        tile = tile_of(FF, 512)

        def part(n, carry):
            at = pl.ds(pl.multiple_of(n * tile, tile), tile)
            v = jnp.dot(
                rows[o].reshape(L * cap, D), w[:, at], preferred_element_type=jnp.float32
            )
            v = v / (1.0 + jnp.exp(-v))
            outs[o, :, :, at] = v.astype(jnp.bfloat16).reshape(L, cap, tile)
            return carry

        lax.fori_loop(0, FF // tile, part, 0)
        for k in range(1, L):
            res_copy(o, k).start()
        keep = pltpu.make_async_copy(outs.at[o, l], res.at[o, l], res_r.at[o, l])
        keep.start()

    def combine(i):
        o = origin(i)
        for k in range(L):
            e = peer(k)
            pltpu.make_async_copy(res.at[o, e], res.at[o, e], res_r.at[o, e]).wait()
        tile = tile_of(FF, 512)
        back = jnp.transpose(comb[o]).astype(jnp.bfloat16)

        def part(n, carry):
            at = pl.ds(pl.multiple_of(n * tile, tile), tile)
            got = jnp.dot(
                back, res[o, :, :, at].reshape(L * cap, tile), preferred_element_type=jnp.float32
            )
            gsum[o, :, at] = got.astype(jnp.bfloat16)
            return carry

        lax.fori_loop(0, FF // tile, part, 0)

        @pl.when(o != g)
        def _():
            gs_copy(o).start()

    def step(i, carry):
        @pl.when(i < G)
        def _():
            arrive(i)

        @pl.when((i >= 1) & (i < G + 1))
        def _():
            @pl.when(i == 1)
            def _():
                load_w.wait()

            expert(i - 1)

        @pl.when(i >= 2)
        def _():
            combine(i - 2)

        return carry

    lax.fori_loop(0, G + 2, step, 0)

    total = gsum[g].astype(jnp.float32)
    for k in range(1, G):
        o = far(k)
        pltpu.make_async_copy(gin.at[o], gin.at[o], gs_r.at[o]).wait()
        total = total + gin[o].astype(jnp.float32)
    out_ref[...] = total.astype(out_ref.dtype)

    for k in range(1, G):
        meta_copy(k).wait_send()
        gs_copy(far(k)).wait_send()

    def drain(o, carry):
        @pl.when((o <= g) & (g < G - 1))
        def _():
            up_copy(o).wait_send()

        @pl.when((o >= g) & (g > 0))
        def _():
            down_copy(o).wait_send()

        for k in range(1, L):
            row_copy(o, k).wait_send()
            res_copy(o, k).wait_send()
        return carry

    lax.fori_loop(0, G, drain, 0)


def everywhere(tokens, routes, gate_weights, w_expert):
    T, D = tokens.shape
    picks = routes.shape[1]
    G = lax.axis_size("group")
    L = lax.axis_size("local")
    cap = T * picks // (G * L)
    FF = w_expert.shape[2]
    meta = jnp.concatenate(
        [routes.T.astype(jnp.float32), gate_weights.T.astype(jnp.float32)], axis=0
    )
    dma = pltpu.SemaphoreType.DMA
    bf16 = jnp.bfloat16
    return pl.pallas_call(
        functools.partial(fused_kernel, G, L, cap),
        out_shape=jax.ShapeDtypeStruct((T, FF), bf16),
        in_specs=[pl.BlockSpec(memory_space=pl.ANY)] * 3,
        out_specs=pl.BlockSpec(memory_space=pltpu.VMEM),
        scratch_shapes=[
            pltpu.VMEM((D, FF), bf16),
            pltpu.VMEM((G, T, D), bf16),
            pltpu.VMEM((G, 2 * picks, T), jnp.float32),
            pltpu.VMEM((G, L * cap, T), bf16),
            pltpu.VMEM((G, L * cap, T), jnp.float32),
            pltpu.VMEM((G, L, cap, D), bf16),
            pltpu.VMEM((G, L, cap, D), bf16),
            pltpu.VMEM((G, L, cap, FF), bf16),
            pltpu.VMEM((G, L, cap, FF), bf16),
            pltpu.VMEM((G, T, FF), bf16),
            pltpu.VMEM((G, T, FF), bf16),
            dma((3,)),
            dma((G,)),
            dma((G,)),
            dma((G,)),
            dma((G,)),
            dma((G,)),
            dma((G, L)),
            dma((G, L)),
            dma((G, L)),
            dma((G, L)),
            dma((G,)),
            dma((G,)),
        ],
        compiler_params=pltpu.CompilerParams(
            collective_id=0, has_side_effects=True, vmem_limit_bytes=58 * 1024 * 1024
        ),
        cost_estimate=pl.CostEstimate(
            flops=2 * T * picks * D * FF, bytes_accessed=2 * D * FF, transcendentals=T * picks * FF
        ),
    )(tokens, meta, w_expert[0])


def solution(mesh):
    groups = mesh.shape["group"]

    def shards(tokens, routes, gate_weights, w_expert):
        if routes.shape[1] == 2 * groups:
            return everywhere(tokens, routes, gate_weights, w_expert)
        return routed(tokens, routes, gate_weights, w_expert)

    return jax.shard_map(
        shards,
        mesh=mesh,
        in_specs=(SPEC, SPEC, SPEC, P(("group", "local"), None, None)),
        out_specs=SPEC,
        check_vma=False,
    )
```

```python
import functools

import jax
import jax.numpy as jnp
from jax import lax
from jax.experimental import pallas as pl
from jax.experimental.pallas import tpu as pltpu
from jax.sharding import PartitionSpec as P

WIDE = 2

SPEC = P(("parts", "group", "local"), None)


def routed(tokens, routes, gate_weights, w_expert):
    tok_rows, picks = routes.shape
    groups = lax.axis_size("group")
    per_group = lax.axis_size("local")
    experts = groups * per_group
    capacity = tok_rows * picks // experts
    weight = w_expert[0]
    gates = gate_weights.astype(jnp.float32)
    group_of = routes // per_group
    pick_ids = jnp.arange(picks, dtype=jnp.int32)
    same = group_of[:, :, None] == group_of[:, None, :]
    others = same & (pick_ids[:, None] != pick_ids[None, :])[None, :, :]
    partner = jnp.sum(jnp.where(others, pick_ids[None, None, :], 0), axis=2)
    earlier = jnp.sum(
        jnp.where(same & (pick_ids[None, :] < pick_ids[:, None])[None, :, :], 1, 0), axis=2
    ).astype(jnp.int32)
    first = (earlier == 0)[:, :, None]
    flat_ids = routes.reshape(-1)
    onehot = (flat_ids[:, None] == jnp.arange(experts, dtype=jnp.int32)[None, :]).astype(jnp.int32)
    before = jnp.cumsum(onehot, axis=0) - onehot
    slot_of = flat_ids * capacity + jnp.sum(before * onehot, axis=1)
    pair_tokens = jnp.arange(tok_rows * picks, dtype=jnp.int32) // picks
    source = jnp.zeros((experts * capacity,), jnp.int32).at[slot_of].set(pair_tokens)
    outgoing = tokens[source]
    arrived = lax.all_to_all(
        outgoing.reshape(experts, capacity, -1),
        ("group", "local"),
        split_axis=0,
        concat_axis=0,
        tiled=True,
    )
    flatrows = arrived.reshape(-1, arrived.shape[-1])
    result = (
        jax.nn.silu(jnp.dot(flatrows, weight, preferred_element_type=jnp.float32))
        .astype(jnp.bfloat16)
        .reshape(experts, capacity, -1)
    )
    returned = lax.all_to_all(result, ("group", "local"), split_axis=0, concat_axis=0, tiled=True)
    pair_out = returned.reshape(experts * capacity, -1)[slot_of].reshape(tok_rows, picks, -1)
    weighted = gates[:, :, None] * pair_out.astype(jnp.float32)
    group_sum = (weighted + jnp.take_along_axis(weighted, partner[:, :, None], axis=1)).astype(
        jnp.bfloat16
    )
    return jnp.sum(
        jnp.where(first, group_sum.astype(jnp.float32), jnp.float32(0.0)), axis=1
    ).astype(jnp.bfloat16)


def tile_of(width, most):
    tile = most
    while width % tile:
        tile -= 128
    return tile


def fused_kernel(
    G, L, cap, W, WF, wide,
    tok_ref, meta_ref, w_ref, out_ref,
    w, tok, tokx, meta, metax, pick, pickx, comb, sel, selx, rows, outs, res, gsum, gin,
    load_sem, meta_s, meta_r, metax_s, metax_r, cross_s,
    up_s, down_s, tok_r, upx_s, downx_s, tokx_r,
    row_s, rowx_s, row_r, res_s, res_r, gs_s, gs_r,
):
    T, D = tok_ref.shape
    FF = w_ref.shape[1]
    C, N, H = D // W, FF // WF, L // 2
    narrow = C - wide
    picks = meta_ref.shape[0] // 2
    g = lax.axis_index("group")
    l = lax.axis_index("local")
    base = l // H * H
    across = lax.rem(l + H, L)

    low = jnp.minimum(g, G - 1 - g)
    side = jnp.where(g < G - 1 - g, 1, -1)

    def origin(i):
        near = (i + 1) // 2 * jnp.where(i % 2 == 1, -1, 1)
        return g + jnp.where(i <= 2 * low, near, (i - low) * side)

    def far(k):
        return lax.rem(g + k, G)

    def mate(k):
        return base + lax.rem(l - base + k, H)

    def away(k):
        return lax.rem(base + H, L) + k

    def remote(src, dst, send, recv, group=None, local=None):
        where = {}
        if group is not None:
            where["group"] = group
        if local is not None:
            where["local"] = local
        return pltpu.make_async_remote_copy(
            src_ref=src, dst_ref=dst, send_sem=send, recv_sem=recv,
            device_id=where, device_id_type=pl.DeviceIdType.MESH,
        )

    def wait_for(ref, sem):
        pltpu.make_async_copy(ref, ref, sem).wait()

    def meta_copy(k):
        return remote(meta.at[g], meta.at[g], meta_s.at[k], meta_r.at[g], group=far(k))

    def metax_copy(k):
        return remote(
            meta.at[g], metax.at[g], metax_s.at[k], metax_r.at[g], group=far(k), local=across
        )

    load_meta = pltpu.make_async_copy(meta_ref, meta.at[g], load_sem.at[0])
    load_w = pltpu.make_async_copy(w_ref, w, load_sem.at[1])
    load_meta.start()
    for c in range(C):
        pltpu.make_async_copy(
            tok_ref.at[:, pl.ds(c * W, W)], tok.at[g, c], tok_r.at[g, c]
        ).start()
    load_w.start()

    barrier = pltpu.get_barrier_semaphore()
    greeted = 0
    for k in range(1, G):
        for where in ({"group": far(k)}, {"group": far(k), "local": across}):
            pl.semaphore_signal(
                barrier, inc=1, device_id=where, device_id_type=pl.DeviceIdType.MESH
            )
            greeted += 1
    for k in range(1, L):
        pl.semaphore_signal(
            barrier, inc=1, device_id={"local": lax.rem(l + k, L)},
            device_id_type=pl.DeviceIdType.MESH,
        )
        greeted += 1
    pl.semaphore_wait(barrier, greeted)

    load_meta.wait()
    if wide:
        metax_copy(0).start()
    for k in range(1, G):
        meta_copy(k).start()
        if wide:
            metax_copy(k).start()

    def places(info, first, count):
        chosen = info[0:picks, :]
        gates = info[picks : 2 * picks, :]
        line = lax.broadcasted_iota(jnp.int32, (picks, T), 0)
        members = jnp.zeros((picks, T), jnp.float32)
        mine, scale = [], []
        for e in range(count):
            hit = chosen == (first + e).astype(jnp.float32)
            mine.append(jnp.sum(jnp.where(hit, 1.0, 0.0), axis=0, keepdims=True))
            scale.append(jnp.sum(jnp.where(hit, gates, 0.0), axis=0, keepdims=True))
            members = members + jnp.where(line == e, mine[e], 0.0)
        ahead = jnp.where(
            lax.broadcasted_iota(jnp.int32, (T, T), 0) < lax.broadcasted_iota(jnp.int32, (T, T), 1),
            1.0, 0.0,
        )
        rank = jnp.dot(members, ahead, preferred_element_type=jnp.float32)
        slot = lax.broadcasted_iota(jnp.int32, (cap, T), 0).astype(jnp.float32)
        here = [
            jnp.where((slot == rank[e : e + 1, :]) & (mine[e] > 0.5), 1.0, 0.0)
            for e in range(count)
        ]
        return here, scale

    def pass_on(buf, o, c, up, down, recv):
        @pl.when((o <= g) & (g < G - 1))
        def _():
            remote(buf.at[o, c], buf.at[o, c], up.at[o], recv.at[o, c], group=g + 1).start()

        @pl.when((o >= g) & (g > 0))
        def _():
            remote(buf.at[o, c], buf.at[o, c], down.at[o], recv.at[o, c], group=g - 1).start()

    def arrive(i):
        o = origin(i)

        @pl.when(o != g)
        def _():
            wait_for(meta.at[o], meta_r.at[o])

        here, scale = places(meta[o], g * L, L)
        for e in range(L):
            pick[o, e * cap : (e + 1) * cap, :] = here[e].astype(jnp.bfloat16)
            comb[o, e * cap : (e + 1) * cap, :] = here[e] * scale[e]

        def chunk(c, carry):
            @pl.when(o != g)
            def _():
                wait_for(tok.at[o, c], tok_r.at[o, c])

            pass_on(tok, o, c, up_s, down_s, tok_r)
            got = jnp.dot(pick[o], tok[o, c], preferred_element_type=jnp.float32)
            sel[o, c] = got.astype(jnp.bfloat16).reshape(L, cap, W)

            @pl.when(c < narrow)
            def _():
                for k in range(H):
                    e = away(k)
                    remote(
                        sel.at[o, c, e], rows.at[o, c, l], row_s.at[o, e], row_r.at[o, l], local=e
                    ).start()

            for k in range(1, H):
                e = mate(k)
                remote(
                    sel.at[o, c, e], rows.at[o, c, l], row_s.at[o, e], row_r.at[o, l], local=e
                ).start()
            rows[o, c, l] = sel[o, c, l]
            return carry

        lax.fori_loop(0, C, chunk, 0)

        if wide:
            wait_for(metax.at[o], metax_r.at[o])
            here, _ = places(metax[o], g * L + base, H)
            for e in range(H):
                pickx[e * cap : (e + 1) * cap, :] = here[e].astype(jnp.bfloat16)

            def chunkx(c, carry):
                wait_for(tokx.at[o, c], tokx_r.at[o, c])
                pass_on(tokx, o, c, upx_s, downx_s, tokx_r)
                got = jnp.dot(pickx[...], tokx[o, c], preferred_element_type=jnp.float32)
                selx[o, c] = got.astype(jnp.bfloat16).reshape(H, cap, W)
                for k in range(1, H):
                    e = mate(k)
                    remote(
                        selx.at[o, c, e - base], rows.at[o, narrow + c, across],
                        rowx_s.at[o, e - base], row_r.at[o, across], local=e,
                    ).start()
                rows[o, narrow + c, across] = selx[o, c, l - base]
                return carry

            lax.fori_loop(0, wide, chunkx, 0)

    def expert(i):
        o = origin(i)
        for k in range(1, H):
            wait_for(rows.at[o, :, mate(k)], row_r.at[o, mate(k)])
            other = lax.rem(mate(k) + H, L)
            wait_for(rows.at[o, :, other], row_r.at[o, other])
        wait_for(rows.at[o, pl.ds(0, narrow), across], row_r.at[o, across])

        def part(n, carry):
            at = pl.ds(pl.multiple_of(n * WF, WF), WF)
            v = jnp.zeros((L * cap, WF), jnp.float32)
            for c in range(C):
                v = v + jnp.dot(
                    rows[o, c].reshape(L * cap, W), w[c * W : (c + 1) * W, at],
                    preferred_element_type=jnp.float32,
                )
            v = v / (1.0 + jnp.exp(-v))
            outs[o, n] = v.astype(jnp.bfloat16).reshape(L, cap, WF)
            for k in range(1, L):
                e = lax.rem(l + k, L)
                remote(
                    outs.at[o, n, e], res.at[o, n, l], res_s.at[o, e], res_r.at[o, n, l], local=e
                ).start()
            res[o, n, l] = outs[o, n, l]
            return carry

        lax.fori_loop(0, N, part, 0)

    def combine(i):
        o = origin(i)
        back = jnp.transpose(comb[o]).astype(jnp.bfloat16)

        def part(n, carry):
            for k in range(1, L):
                e = lax.rem(l + k, L)
                wait_for(res.at[o, n, e], res_r.at[o, n, e])
            got = jnp.dot(
                back, res[o, n].reshape(L * cap, WF), preferred_element_type=jnp.float32
            )
            gsum[o, n] = got.astype(jnp.bfloat16)

            @pl.when(o != g)
            def _():
                remote(
                    gsum.at[o, n], gin.at[g, n], gs_s.at[o], gs_r.at[g, n], group=o
                ).start()

            return carry

        lax.fori_loop(0, N, part, 0)

    for c in range(C):
        wait_for(tok.at[g, c], tok_r.at[g, c])
    for c in range(wide):
        remote(
            tok.at[g, narrow + c], tokx.at[g, c], cross_s, tokx_r.at[g, c], local=across
        ).start()

    def step(i, carry):
        @pl.when(i < G)
        def _():
            arrive(i)

        @pl.when((i >= 1) & (i < G + 1))
        def _():
            @pl.when(i == 1)
            def _():
                load_w.wait()

            expert(i - 1)

        @pl.when(i >= 2)
        def _():
            combine(i - 2)

        return carry

    lax.fori_loop(0, G + 2, step, 0)

    for n in range(N):
        total = gsum[g, n].astype(jnp.float32)
        for k in range(1, G):
            o = far(k)
            wait_for(gin.at[o, n], gs_r.at[o, n])
            total = total + gin[o, n].astype(jnp.float32)
        out_ref[:, n * WF : (n + 1) * WF] = total.astype(out_ref.dtype)

    if wide:
        metax_copy(0).wait_send()
    for k in range(1, G):
        meta_copy(k).wait_send()
        if wide:
            metax_copy(k).wait_send()
        wait_for(gsum.at[far(k)], gs_s.at[far(k)])
    if wide:
        wait_for(tokx.at[g], cross_s)

    def drain(o, carry):
        @pl.when((o <= g) & (g < G - 1))
        def _():
            wait_for(tok.at[o], up_s.at[o])
            if wide:
                wait_for(tokx.at[o], upx_s.at[o])

        @pl.when((o >= g) & (g > 0))
        def _():
            wait_for(tok.at[o], down_s.at[o])
            if wide:
                wait_for(tokx.at[o], downx_s.at[o])

        for k in range(H):
            wait_for(sel.at[o, pl.ds(0, narrow), away(k)], row_s.at[o, away(k)])
        for k in range(1, H):
            wait_for(sel.at[o, :, mate(k)], row_s.at[o, mate(k)])
            if wide:
                wait_for(selx.at[o, :, mate(k) - base], rowx_s.at[o, mate(k) - base])
        for k in range(1, L):
            e = lax.rem(l + k, L)
            wait_for(outs.at[o, :, e], res_s.at[o, e])
        return carry

    lax.fori_loop(0, G, drain, 0)


def everywhere(tokens, routes, gate_weights, w_expert):
    T, D = tokens.shape
    picks = routes.shape[1]
    G = lax.axis_size("group")
    L = lax.axis_size("local")
    cap = T * picks // (G * L)
    FF = w_expert.shape[2]
    W, WF = tile_of(D, 512), tile_of(FF, 512)
    C, N, H = D // W, FF // WF, L // 2
    wide = C * WIDE // 7
    some = max(wide, 1)
    meta = jnp.concatenate(
        [routes.T.astype(jnp.float32), gate_weights.T.astype(jnp.float32)], axis=0
    )
    dma = pltpu.SemaphoreType.DMA
    bf16 = jnp.bfloat16
    return pl.pallas_call(
        functools.partial(fused_kernel, G, L, cap, W, WF, wide),
        out_shape=jax.ShapeDtypeStruct((T, FF), bf16),
        in_specs=[pl.BlockSpec(memory_space=pl.ANY)] * 3,
        out_specs=pl.BlockSpec(memory_space=pltpu.VMEM),
        scratch_shapes=[
            pltpu.VMEM((D, FF), bf16),
            pltpu.VMEM((G, C, T, W), bf16),
            pltpu.VMEM((G, some, T, W), bf16),
            pltpu.VMEM((G, 2 * picks, T), jnp.float32),
            pltpu.VMEM((G, 2 * picks, T), jnp.float32),
            pltpu.VMEM((G, L * cap, T), bf16),
            pltpu.VMEM((H * cap, T), bf16),
            pltpu.VMEM((G, L * cap, T), jnp.float32),
            pltpu.VMEM((G, C, L, cap, W), bf16),
            pltpu.VMEM((G, some, H, cap, W), bf16),
            pltpu.VMEM((G, C, L, cap, W), bf16),
            pltpu.VMEM((G, N, L, cap, WF), bf16),
            pltpu.VMEM((G, N, L, cap, WF), bf16),
            pltpu.VMEM((G, N, T, WF), bf16),
            pltpu.VMEM((G, N, T, WF), bf16),
            dma((2,)),
            dma((G,)),
            dma((G,)),
            dma((G,)),
            dma((G,)),
            dma,
            dma((G,)),
            dma((G,)),
            dma((G, C)),
            dma((G,)),
            dma((G,)),
            dma((G, some)),
            dma((G, L)),
            dma((G, H)),
            dma((G, L)),
            dma((G, L)),
            dma((G, N, L)),
            dma((G,)),
            dma((G, N)),
        ],
        compiler_params=pltpu.CompilerParams(
            collective_id=0, has_side_effects=True, vmem_limit_bytes=58 * 1024 * 1024
        ),
        cost_estimate=pl.CostEstimate(
            flops=2 * T * picks * D * FF, bytes_accessed=2 * D * FF, transcendentals=T * picks * FF
        ),
    )(tokens, meta, w_expert[0])


def solution(mesh):
    groups = mesh.shape["group"]

    def shards(tokens, routes, gate_weights, w_expert):
        if routes.shape[1] == 2 * groups:
            return everywhere(tokens, routes, gate_weights, w_expert)
        return routed(tokens, routes, gate_weights, w_expert)

    return jax.shard_map(
        shards,
        mesh=mesh,
        in_specs=(SPEC, SPEC, SPEC, P(("group", "local"), None, None)),
        out_specs=SPEC,
        check_vma=False,
    )
```

```python
import functools

import jax
import jax.numpy as jnp
from jax import lax
from jax.experimental import pallas as pl
from jax.experimental.pallas import tpu as pltpu
from jax.sharding import PartitionSpec as P

WIDE = 5

SPEC = P(("parts", "group", "local"), None)


def routed(tokens, routes, gate_weights, w_expert):
    tok_rows, picks = routes.shape
    groups = lax.axis_size("group")
    per_group = lax.axis_size("local")
    experts = groups * per_group
    capacity = tok_rows * picks // experts
    weight = w_expert[0]
    gates = gate_weights.astype(jnp.float32)
    group_of = routes // per_group
    pick_ids = jnp.arange(picks, dtype=jnp.int32)
    same = group_of[:, :, None] == group_of[:, None, :]
    others = same & (pick_ids[:, None] != pick_ids[None, :])[None, :, :]
    partner = jnp.sum(jnp.where(others, pick_ids[None, None, :], 0), axis=2)
    earlier = jnp.sum(
        jnp.where(same & (pick_ids[None, :] < pick_ids[:, None])[None, :, :], 1, 0), axis=2
    ).astype(jnp.int32)
    first = (earlier == 0)[:, :, None]
    flat_ids = routes.reshape(-1)
    onehot = (flat_ids[:, None] == jnp.arange(experts, dtype=jnp.int32)[None, :]).astype(jnp.int32)
    before = jnp.cumsum(onehot, axis=0) - onehot
    slot_of = flat_ids * capacity + jnp.sum(before * onehot, axis=1)
    pair_tokens = jnp.arange(tok_rows * picks, dtype=jnp.int32) // picks
    source = jnp.zeros((experts * capacity,), jnp.int32).at[slot_of].set(pair_tokens)
    outgoing = tokens[source]
    arrived = lax.all_to_all(
        outgoing.reshape(experts, capacity, -1),
        ("group", "local"),
        split_axis=0,
        concat_axis=0,
        tiled=True,
    )
    flatrows = arrived.reshape(-1, arrived.shape[-1])
    result = (
        jax.nn.silu(jnp.dot(flatrows, weight, preferred_element_type=jnp.float32))
        .astype(jnp.bfloat16)
        .reshape(experts, capacity, -1)
    )
    returned = lax.all_to_all(result, ("group", "local"), split_axis=0, concat_axis=0, tiled=True)
    pair_out = returned.reshape(experts * capacity, -1)[slot_of].reshape(tok_rows, picks, -1)
    weighted = gates[:, :, None] * pair_out.astype(jnp.float32)
    group_sum = (weighted + jnp.take_along_axis(weighted, partner[:, :, None], axis=1)).astype(
        jnp.bfloat16
    )
    return jnp.sum(
        jnp.where(first, group_sum.astype(jnp.float32), jnp.float32(0.0)), axis=1
    ).astype(jnp.bfloat16)


def tile_of(width, most):
    tile = most
    while width % tile:
        tile -= 128
    return tile


def fused_kernel(
    G, L, cap, W, WF, wide,
    tok_ref, meta_ref, w_ref, out_ref,
    w, tok, tokx, meta, metax, pick, pickx, comb, sel, selx, rows, outs, res, gsum, gin,
    load_sem, meta_s, meta_r, metax_s, metax_r, cross_s,
    up_s, down_s, tok_r, upx_s, downx_s, tokx_r,
    row_s, rowx_s, row_r, res_s, res_r, gs_s, gs_r,
):
    T, D = tok_ref.shape
    FF = w_ref.shape[1]
    C, N, H = D // W, FF // WF, L // 2
    narrow = C - wide
    picks = meta_ref.shape[0] // 2
    g = lax.axis_index("group")
    l = lax.axis_index("local")
    base = l // H * H
    across = lax.rem(l + H, L)

    low = jnp.minimum(g, G - 1 - g)
    side = jnp.where(g < G - 1 - g, 1, -1)

    def origin(i):
        near = (i + 1) // 2 * jnp.where(i % 2 == 1, -1, 1)
        return g + jnp.where(i <= 2 * low, near, (i - low) * side)

    def far(k):
        return lax.rem(g + k, G)

    def mate(k):
        return base + lax.rem(l - base + k, H)

    def away(k):
        return lax.rem(base + H, L) + k

    def remote(src, dst, send, recv, group=None, local=None):
        where = {}
        if group is not None:
            where["group"] = group
        if local is not None:
            where["local"] = local
        return pltpu.make_async_remote_copy(
            src_ref=src, dst_ref=dst, send_sem=send, recv_sem=recv,
            device_id=where, device_id_type=pl.DeviceIdType.MESH,
        )

    def wait_for(ref, sem):
        pltpu.make_async_copy(ref, ref, sem).wait()

    def meta_copy(k):
        return remote(meta.at[g], meta.at[g], meta_s.at[k], meta_r.at[g], group=far(k))

    def metax_copy(k):
        return remote(
            meta.at[g], metax.at[g], metax_s.at[k], metax_r.at[g], group=far(k), local=across
        )

    load_meta = pltpu.make_async_copy(meta_ref, meta.at[g], load_sem.at[0])
    load_w = pltpu.make_async_copy(w_ref, w, load_sem.at[1])
    load_meta.start()
    for c in range(C):
        pltpu.make_async_copy(
            tok_ref.at[:, pl.ds(c * W, W)], tok.at[g, c], tok_r.at[g, c]
        ).start()
    load_w.start()

    barrier = pltpu.get_barrier_semaphore()
    greeted = 0
    for k in range(1, G):
        for where in ({"group": far(k)}, {"group": far(k), "local": across}):
            pl.semaphore_signal(
                barrier, inc=1, device_id=where, device_id_type=pl.DeviceIdType.MESH
            )
            greeted += 1
    for k in range(1, L):
        pl.semaphore_signal(
            barrier, inc=1, device_id={"local": lax.rem(l + k, L)},
            device_id_type=pl.DeviceIdType.MESH,
        )
        greeted += 1
    pl.semaphore_wait(barrier, greeted)

    load_meta.wait()
    if wide:
        metax_copy(0).start()
    for k in range(1, G):
        meta_copy(k).start()
        if wide:
            metax_copy(k).start()

    def places(info, first, count):
        chosen = info[0:picks, :]
        gates = info[picks : 2 * picks, :]
        line = lax.broadcasted_iota(jnp.int32, (picks, T), 0)
        members = jnp.zeros((picks, T), jnp.float32)
        mine, scale = [], []
        for e in range(count):
            hit = chosen == (first + e).astype(jnp.float32)
            mine.append(jnp.sum(jnp.where(hit, 1.0, 0.0), axis=0, keepdims=True))
            scale.append(jnp.sum(jnp.where(hit, gates, 0.0), axis=0, keepdims=True))
            members = members + jnp.where(line == e, mine[e], 0.0)
        ahead = jnp.where(
            lax.broadcasted_iota(jnp.int32, (T, T), 0) < lax.broadcasted_iota(jnp.int32, (T, T), 1),
            1.0, 0.0,
        )
        rank = jnp.dot(members, ahead, preferred_element_type=jnp.float32)
        slot = lax.broadcasted_iota(jnp.int32, (cap, T), 0).astype(jnp.float32)
        here = [
            jnp.where((slot == rank[e : e + 1, :]) & (mine[e] > 0.5), 1.0, 0.0)
            for e in range(count)
        ]
        return here, scale

    def pass_on(buf, o, c, up, down, recv):
        @pl.when((o <= g) & (g < G - 1))
        def _():
            remote(buf.at[o, c], buf.at[o, c], up.at[o], recv.at[o, c], group=g + 1).start()

        @pl.when((o >= g) & (g > 0))
        def _():
            remote(buf.at[o, c], buf.at[o, c], down.at[o], recv.at[o, c], group=g - 1).start()

    def arrive(i):
        o = origin(i)

        @pl.when(o != g)
        def _():
            wait_for(meta.at[o], meta_r.at[o])

        here, scale = places(meta[o], g * L, L)
        for e in range(L):
            pick[o, e * cap : (e + 1) * cap, :] = here[e].astype(jnp.bfloat16)
            comb[o, e * cap : (e + 1) * cap, :] = here[e] * scale[e]

        def chunk(c, carry):
            @pl.when(o != g)
            def _():
                wait_for(tok.at[o, c], tok_r.at[o, c])

            pass_on(tok, o, c, up_s, down_s, tok_r)
            got = jnp.dot(pick[o], tok[o, c], preferred_element_type=jnp.float32)
            sel[o, c] = got.astype(jnp.bfloat16).reshape(L, cap, W)

            @pl.when(c < narrow)
            def _():
                for k in range(H):
                    e = away(k)
                    remote(
                        sel.at[o, c, e], rows.at[o, c, l], row_s.at[o, e], row_r.at[o, l], local=e
                    ).start()

            for k in range(1, H):
                e = mate(k)
                remote(
                    sel.at[o, c, e], rows.at[o, c, l], row_s.at[o, e], row_r.at[o, l], local=e
                ).start()
            rows[o, c, l] = sel[o, c, l]
            return carry

        lax.fori_loop(0, C, chunk, 0)

        if wide:
            wait_for(metax.at[o], metax_r.at[o])
            here, _ = places(metax[o], g * L + base, H)
            for e in range(H):
                pickx[e * cap : (e + 1) * cap, :] = here[e].astype(jnp.bfloat16)

            def chunkx(c, carry):
                wait_for(tokx.at[o, c], tokx_r.at[o, c])
                pass_on(tokx, o, c, upx_s, downx_s, tokx_r)
                got = jnp.dot(pickx[...], tokx[o, c], preferred_element_type=jnp.float32)
                selx[o, c] = got.astype(jnp.bfloat16).reshape(H, cap, W)
                for k in range(1, H):
                    e = mate(k)
                    remote(
                        selx.at[o, c, e - base], rows.at[o, narrow + c, across],
                        rowx_s.at[o, e - base], row_r.at[o, across], local=e,
                    ).start()
                rows[o, narrow + c, across] = selx[o, c, l - base]
                return carry

            lax.fori_loop(0, wide, chunkx, 0)

    def expert(i):
        o = origin(i)
        for k in range(1, H):
            wait_for(rows.at[o, :, mate(k)], row_r.at[o, mate(k)])
            other = lax.rem(mate(k) + H, L)
            wait_for(rows.at[o, :, other], row_r.at[o, other])
        wait_for(rows.at[o, pl.ds(0, narrow), across], row_r.at[o, across])

        def part(n, carry):
            at = pl.ds(pl.multiple_of(n * WF, WF), WF)
            v = jnp.zeros((L * cap, WF), jnp.float32)
            for c in range(C):
                v = v + jnp.dot(
                    rows[o, c].reshape(L * cap, W), w[c * W : (c + 1) * W, at],
                    preferred_element_type=jnp.float32,
                )
            v = v / (1.0 + jnp.exp(-v))
            outs[o, n] = v.astype(jnp.bfloat16).reshape(L, cap, WF)
            for k in range(1, L):
                e = lax.rem(l + k, L)
                remote(
                    outs.at[o, n, e], res.at[o, n, l], res_s.at[o, e], res_r.at[o, n, l], local=e
                ).start()
            res[o, n, l] = outs[o, n, l]
            return carry

        lax.fori_loop(0, N, part, 0)

    def combine(i):
        o = origin(i)
        back = jnp.transpose(comb[o]).astype(jnp.bfloat16)

        def part(n, carry):
            for k in range(1, L):
                e = lax.rem(l + k, L)
                wait_for(res.at[o, n, e], res_r.at[o, n, e])
            got = jnp.dot(
                back, res[o, n].reshape(L * cap, WF), preferred_element_type=jnp.float32
            )
            gsum[o, n] = got.astype(jnp.bfloat16)

            @pl.when(o != g)
            def _():
                remote(
                    gsum.at[o, n], gin.at[g, n], gs_s.at[o], gs_r.at[g, n], group=o
                ).start()

            return carry

        lax.fori_loop(0, N, part, 0)

    for c in range(C):
        wait_for(tok.at[g, c], tok_r.at[g, c])
    for c in range(wide):
        remote(
            tok.at[g, narrow + c], tokx.at[g, c], cross_s, tokx_r.at[g, c], local=across
        ).start()

    def step(i, carry):
        @pl.when(i < G)
        def _():
            arrive(i)

        @pl.when((i >= 1) & (i < G + 1))
        def _():
            @pl.when(i == 1)
            def _():
                load_w.wait()

            expert(i - 1)

        @pl.when(i >= 2)
        def _():
            combine(i - 2)

        return carry

    lax.fori_loop(0, G + 2, step, 0)

    for n in range(N):
        total = gsum[g, n].astype(jnp.float32)
        for k in range(1, G):
            o = far(k)
            wait_for(gin.at[o, n], gs_r.at[o, n])
            total = total + gin[o, n].astype(jnp.float32)
        out_ref[:, n * WF : (n + 1) * WF] = total.astype(out_ref.dtype)

    if wide:
        metax_copy(0).wait_send()
    for k in range(1, G):
        meta_copy(k).wait_send()
        if wide:
            metax_copy(k).wait_send()
        wait_for(gsum.at[far(k)], gs_s.at[far(k)])
    if wide:
        wait_for(tokx.at[g], cross_s)

    def drain(o, carry):
        @pl.when((o <= g) & (g < G - 1))
        def _():
            wait_for(tok.at[o], up_s.at[o])
            if wide:
                wait_for(tokx.at[o], upx_s.at[o])

        @pl.when((o >= g) & (g > 0))
        def _():
            wait_for(tok.at[o], down_s.at[o])
            if wide:
                wait_for(tokx.at[o], downx_s.at[o])

        for k in range(H):
            wait_for(sel.at[o, pl.ds(0, narrow), away(k)], row_s.at[o, away(k)])
        for k in range(1, H):
            wait_for(sel.at[o, :, mate(k)], row_s.at[o, mate(k)])
            if wide:
                wait_for(selx.at[o, :, mate(k) - base], rowx_s.at[o, mate(k) - base])
        for k in range(1, L):
            e = lax.rem(l + k, L)
            wait_for(outs.at[o, :, e], res_s.at[o, e])
        return carry

    lax.fori_loop(0, G, drain, 0)


def everywhere(tokens, routes, gate_weights, w_expert):
    T, D = tokens.shape
    picks = routes.shape[1]
    G = lax.axis_size("group")
    L = lax.axis_size("local")
    cap = T * picks // (G * L)
    FF = w_expert.shape[2]
    W, WF = tile_of(D, 256), tile_of(FF, 512)
    C, N, H = D // W, FF // WF, L // 2
    wide = C * WIDE // 14
    some = max(wide, 1)
    meta = jnp.concatenate(
        [routes.T.astype(jnp.float32), gate_weights.T.astype(jnp.float32)], axis=0
    )
    dma = pltpu.SemaphoreType.DMA
    bf16 = jnp.bfloat16
    return pl.pallas_call(
        functools.partial(fused_kernel, G, L, cap, W, WF, wide),
        out_shape=jax.ShapeDtypeStruct((T, FF), bf16),
        in_specs=[pl.BlockSpec(memory_space=pl.ANY)] * 3,
        out_specs=pl.BlockSpec(memory_space=pltpu.VMEM),
        scratch_shapes=[
            pltpu.VMEM((D, FF), bf16),
            pltpu.VMEM((G, C, T, W), bf16),
            pltpu.VMEM((G, some, T, W), bf16),
            pltpu.VMEM((G, 2 * picks, T), jnp.float32),
            pltpu.VMEM((G, 2 * picks, T), jnp.float32),
            pltpu.VMEM((G, L * cap, T), bf16),
            pltpu.VMEM((H * cap, T), bf16),
            pltpu.VMEM((G, L * cap, T), jnp.float32),
            pltpu.VMEM((G, C, L, cap, W), bf16),
            pltpu.VMEM((G, some, H, cap, W), bf16),
            pltpu.VMEM((G, C, L, cap, W), bf16),
            pltpu.VMEM((G, N, L, cap, WF), bf16),
            pltpu.VMEM((G, N, L, cap, WF), bf16),
            pltpu.VMEM((G, N, T, WF), bf16),
            pltpu.VMEM((G, N, T, WF), bf16),
            dma((2,)),
            dma((G,)),
            dma((G,)),
            dma((G,)),
            dma((G,)),
            dma,
            dma((G,)),
            dma((G,)),
            dma((G, C)),
            dma((G,)),
            dma((G,)),
            dma((G, some)),
            dma((G, L)),
            dma((G, H)),
            dma((G, L)),
            dma((G, L)),
            dma((G, N, L)),
            dma((G,)),
            dma((G, N)),
        ],
        compiler_params=pltpu.CompilerParams(
            collective_id=0, has_side_effects=True, vmem_limit_bytes=58 * 1024 * 1024
        ),
        cost_estimate=pl.CostEstimate(
            flops=2 * T * picks * D * FF, bytes_accessed=2 * D * FF, transcendentals=T * picks * FF
        ),
    )(tokens, meta, w_expert[0])


def solution(mesh):
    groups = mesh.shape["group"]

    def shards(tokens, routes, gate_weights, w_expert):
        if routes.shape[1] == 2 * groups:
            return everywhere(tokens, routes, gate_weights, w_expert)
        return routed(tokens, routes, gate_weights, w_expert)

    return jax.shard_map(
        shards,
        mesh=mesh,
        in_specs=(SPEC, SPEC, SPEC, P(("group", "local"), None, None)),
        out_specs=SPEC,
        check_vma=False,
    )
```

```python
import functools

import jax
import jax.numpy as jnp
from jax import lax
from jax.experimental import pallas as pl
from jax.experimental.pallas import tpu as pltpu
from jax.sharding import PartitionSpec as P

WIDE = 5

SPEC = P(("parts", "group", "local"), None)


def routed(tokens, routes, gate_weights, w_expert):
    tok_rows, picks = routes.shape
    groups = lax.axis_size("group")
    per_group = lax.axis_size("local")
    experts = groups * per_group
    capacity = tok_rows * picks // experts
    weight = w_expert[0]
    gates = gate_weights.astype(jnp.float32)
    group_of = routes // per_group
    pick_ids = jnp.arange(picks, dtype=jnp.int32)
    same = group_of[:, :, None] == group_of[:, None, :]
    others = same & (pick_ids[:, None] != pick_ids[None, :])[None, :, :]
    partner = jnp.sum(jnp.where(others, pick_ids[None, None, :], 0), axis=2)
    earlier = jnp.sum(
        jnp.where(same & (pick_ids[None, :] < pick_ids[:, None])[None, :, :], 1, 0), axis=2
    ).astype(jnp.int32)
    first = (earlier == 0)[:, :, None]
    flat_ids = routes.reshape(-1)
    onehot = (flat_ids[:, None] == jnp.arange(experts, dtype=jnp.int32)[None, :]).astype(jnp.int32)
    before = jnp.cumsum(onehot, axis=0) - onehot
    slot_of = flat_ids * capacity + jnp.sum(before * onehot, axis=1)
    pair_tokens = jnp.arange(tok_rows * picks, dtype=jnp.int32) // picks
    source = jnp.zeros((experts * capacity,), jnp.int32).at[slot_of].set(pair_tokens)
    outgoing = tokens[source]
    arrived = lax.all_to_all(
        outgoing.reshape(experts, capacity, -1),
        ("group", "local"),
        split_axis=0,
        concat_axis=0,
        tiled=True,
    )
    flatrows = arrived.reshape(-1, arrived.shape[-1])
    result = (
        jax.nn.silu(jnp.dot(flatrows, weight, preferred_element_type=jnp.float32))
        .astype(jnp.bfloat16)
        .reshape(experts, capacity, -1)
    )
    returned = lax.all_to_all(result, ("group", "local"), split_axis=0, concat_axis=0, tiled=True)
    pair_out = returned.reshape(experts * capacity, -1)[slot_of].reshape(tok_rows, picks, -1)
    weighted = gates[:, :, None] * pair_out.astype(jnp.float32)
    group_sum = (weighted + jnp.take_along_axis(weighted, partner[:, :, None], axis=1)).astype(
        jnp.bfloat16
    )
    return jnp.sum(
        jnp.where(first, group_sum.astype(jnp.float32), jnp.float32(0.0)), axis=1
    ).astype(jnp.bfloat16)


def tile_of(width, most):
    tile = most
    while width % tile:
        tile -= 128
    return tile


def fused_kernel(
    G, L, cap, W, WF, wide,
    tok_ref, meta_ref, w_ref, out_ref,
    w, tok, tokx, meta, metax, pick, pickx, comb, sel, selx, rows, outs, res, gsum, gin,
    load_sem, meta_s, meta_r, metax_s, metax_r, cross_s,
    up_s, down_s, tok_r, upx_s, downx_s, tokx_r,
    row_s, rowx_s, row_r, res_s, res_r, gs_s, gs_r,
):
    T, D = tok_ref.shape
    FF = w_ref.shape[1]
    C, N, H = D // W, FF // WF, L // 2
    narrow = C - wide
    picks = meta_ref.shape[0] // 2
    g = lax.axis_index("group")
    l = lax.axis_index("local")
    base = l // H * H
    across = lax.rem(l + H, L)

    low = jnp.minimum(g, G - 1 - g)
    side = jnp.where(g < G - 1 - g, 1, -1)

    def origin(i):
        near = (i + 1) // 2 * jnp.where(i % 2 == 1, -1, 1)
        return g + jnp.where(i <= 2 * low, near, (i - low) * side)

    def far(k):
        return lax.rem(g + k, G)

    def mate(k):
        return base + lax.rem(l - base + k, H)

    def away(k):
        return lax.rem(base + H, L) + k

    def remote(src, dst, send, recv, group=None, local=None):
        where = {}
        if group is not None:
            where["group"] = group
        if local is not None:
            where["local"] = local
        return pltpu.make_async_remote_copy(
            src_ref=src, dst_ref=dst, send_sem=send, recv_sem=recv,
            device_id=where, device_id_type=pl.DeviceIdType.MESH,
        )

    def wait_for(ref, sem):
        pltpu.make_async_copy(ref, ref, sem).wait()

    def meta_copy(k):
        return remote(meta.at[g], meta.at[g], meta_s.at[k], meta_r.at[g], group=far(k))

    def metax_copy(k):
        return remote(
            meta.at[g], metax.at[g], metax_s.at[k], metax_r.at[g], group=far(k), local=across
        )

    load_meta = pltpu.make_async_copy(meta_ref, meta.at[g], load_sem.at[0])
    load_w = pltpu.make_async_copy(w_ref, w, load_sem.at[1])
    load_meta.start()
    for c in range(C):
        pltpu.make_async_copy(
            tok_ref.at[:, pl.ds(c * W, W)], tok.at[g, c], tok_r.at[g, c]
        ).start()
    load_w.start()

    barrier = pltpu.get_barrier_semaphore()
    greeted = 0
    for k in range(1, G):
        for where in ({"group": far(k)}, {"group": far(k), "local": across}):
            pl.semaphore_signal(
                barrier, inc=1, device_id=where, device_id_type=pl.DeviceIdType.MESH
            )
            greeted += 1
    for k in range(1, L):
        pl.semaphore_signal(
            barrier, inc=1, device_id={"local": lax.rem(l + k, L)},
            device_id_type=pl.DeviceIdType.MESH,
        )
        greeted += 1
    pl.semaphore_wait(barrier, greeted)

    load_meta.wait()
    if wide:
        metax_copy(0).start()
    for k in range(1, G):
        meta_copy(k).start()
        if wide:
            metax_copy(k).start()

    def places(info, first, count):
        chosen = info[0:picks, :]
        gates = info[picks : 2 * picks, :]
        line = lax.broadcasted_iota(jnp.int32, (picks, T), 0)
        members = jnp.zeros((picks, T), jnp.float32)
        mine, scale = [], []
        for e in range(count):
            hit = chosen == (first + e).astype(jnp.float32)
            mine.append(jnp.sum(jnp.where(hit, 1.0, 0.0), axis=0, keepdims=True))
            scale.append(jnp.sum(jnp.where(hit, gates, 0.0), axis=0, keepdims=True))
            members = members + jnp.where(line == e, mine[e], 0.0)
        ahead = jnp.where(
            lax.broadcasted_iota(jnp.int32, (T, T), 0) < lax.broadcasted_iota(jnp.int32, (T, T), 1),
            1.0, 0.0,
        )
        rank = jnp.dot(members, ahead, preferred_element_type=jnp.float32)
        slot = lax.broadcasted_iota(jnp.int32, (cap, T), 0).astype(jnp.float32)
        here = [
            jnp.where((slot == rank[e : e + 1, :]) & (mine[e] > 0.5), 1.0, 0.0)
            for e in range(count)
        ]
        return here, scale

    def pass_on(buf, o, c, up, down, recv):
        @pl.when((o <= g) & (g < G - 1))
        def _():
            remote(buf.at[o, c], buf.at[o, c], up.at[o], recv.at[o, c], group=g + 1).start()

        @pl.when((o >= g) & (g > 0))
        def _():
            remote(buf.at[o, c], buf.at[o, c], down.at[o], recv.at[o, c], group=g - 1).start()

    def arrive(i):
        o = origin(i)

        @pl.when(o != g)
        def _():
            wait_for(meta.at[o], meta_r.at[o])

        here, scale = places(meta[o], g * L, L)
        for e in range(L):
            pick[o, e * cap : (e + 1) * cap, :] = here[e].astype(jnp.bfloat16)
            comb[o, e * cap : (e + 1) * cap, :] = here[e] * scale[e]

        def chunk(c, carry):
            @pl.when(o != g)
            def _():
                wait_for(tok.at[o, c], tok_r.at[o, c])

            pass_on(tok, o, c, up_s, down_s, tok_r)
            got = jnp.dot(pick[o], tok[o, c], preferred_element_type=jnp.float32)
            sel[o, c] = got.astype(jnp.bfloat16).reshape(L, cap, W)

            @pl.when(c < narrow)
            def _():
                for k in range(H):
                    e = away(k)
                    remote(
                        sel.at[o, c, e], rows.at[o, c, l], row_s.at[o, e], row_r.at[o, l], local=e
                    ).start()

            for k in range(1, H):
                e = mate(k)
                remote(
                    sel.at[o, c, e], rows.at[o, c, l], row_s.at[o, e], row_r.at[o, l], local=e
                ).start()
            rows[o, c, l] = sel[o, c, l]
            return carry

        lax.fori_loop(0, C, chunk, 0)

        if wide:
            wait_for(metax.at[o], metax_r.at[o])
            here, _ = places(metax[o], g * L + base, H)
            for e in range(H):
                pickx[e * cap : (e + 1) * cap, :] = here[e].astype(jnp.bfloat16)

            def chunkx(c, carry):
                wait_for(tokx.at[o, c], tokx_r.at[o, c])
                pass_on(tokx, o, c, upx_s, downx_s, tokx_r)
                got = jnp.dot(pickx[...], tokx[o, c], preferred_element_type=jnp.float32)
                selx[o, c] = got.astype(jnp.bfloat16).reshape(H, cap, W)
                for k in range(1, H):
                    e = mate(k)
                    remote(
                        selx.at[o, c, e - base], rows.at[o, narrow + c, across],
                        rowx_s.at[o, e - base], row_r.at[o, across], local=e,
                    ).start()
                rows[o, narrow + c, across] = selx[o, c, l - base]
                return carry

            lax.fori_loop(0, wide, chunkx, 0)

    def expert(i):
        o = origin(i)
        for k in range(1, H):
            wait_for(rows.at[o, :, mate(k)], row_r.at[o, mate(k)])
            other = lax.rem(mate(k) + H, L)
            wait_for(rows.at[o, :, other], row_r.at[o, other])
        wait_for(rows.at[o, pl.ds(0, narrow), across], row_r.at[o, across])

        def part(n, carry):
            at = pl.ds(pl.multiple_of(n * WF, WF), WF)
            v = jnp.zeros((L * cap, WF), jnp.float32)
            for c in range(C):
                v = v + jnp.dot(
                    rows[o, c].reshape(L * cap, W), w[c * W : (c + 1) * W, at],
                    preferred_element_type=jnp.float32,
                )
            v = v / (1.0 + jnp.exp(-v))
            outs[o, n] = v.astype(jnp.bfloat16).reshape(L, cap, WF)
            for k in range(1, L):
                e = lax.rem(l + k, L)
                remote(
                    outs.at[o, n, e], res.at[o, n, l], res_s.at[o, e], res_r.at[o, n, l], local=e
                ).start()
            res[o, n, l] = outs[o, n, l]
            return carry

        lax.fori_loop(0, N, part, 0)

    def combine(i):
        o = origin(i)
        back = jnp.transpose(comb[o]).astype(jnp.bfloat16)

        def part(n, carry):
            for k in range(1, L):
                e = lax.rem(l + k, L)
                wait_for(res.at[o, n, e], res_r.at[o, n, e])
            got = jnp.dot(
                back, res[o, n].reshape(L * cap, WF), preferred_element_type=jnp.float32
            )
            gsum[o, n] = got.astype(jnp.bfloat16)

            @pl.when(o != g)
            def _():
                remote(
                    gsum.at[o, n], gin.at[g, n], gs_s.at[o], gs_r.at[g, n], group=o
                ).start()

            return carry

        lax.fori_loop(0, N, part, 0)

    for c in range(C):
        wait_for(tok.at[g, c], tok_r.at[g, c])
    for c in range(wide):
        remote(
            tok.at[g, narrow + c], tokx.at[g, c], cross_s, tokx_r.at[g, c], local=across
        ).start()

    def step(i, carry):
        @pl.when(i < G)
        def _():
            arrive(i)

        @pl.when((i >= 1) & (i < G + 1))
        def _():
            @pl.when(i == 1)
            def _():
                load_w.wait()

            expert(i - 1)

        @pl.when(i >= 2)
        def _():
            combine(i - 2)

        return carry

    lax.fori_loop(0, G + 2, step, 0)

    for n in range(N):
        total = gsum[g, n].astype(jnp.float32)
        for k in range(1, G):
            o = far(k)
            wait_for(gin.at[o, n], gs_r.at[o, n])
            total = total + gin[o, n].astype(jnp.float32)
        out_ref[:, n * WF : (n + 1) * WF] = total.astype(out_ref.dtype)

    if wide:
        metax_copy(0).wait_send()
    for k in range(1, G):
        meta_copy(k).wait_send()
        if wide:
            metax_copy(k).wait_send()
        wait_for(gsum.at[far(k)], gs_s.at[far(k)])
    if wide:
        wait_for(tokx.at[g], cross_s)

    def drain(o, carry):
        @pl.when((o <= g) & (g < G - 1))
        def _():
            wait_for(tok.at[o], up_s.at[o])
            if wide:
                wait_for(tokx.at[o], upx_s.at[o])

        @pl.when((o >= g) & (g > 0))
        def _():
            wait_for(tok.at[o], down_s.at[o])
            if wide:
                wait_for(tokx.at[o], downx_s.at[o])

        for k in range(H):
            wait_for(sel.at[o, pl.ds(0, narrow), away(k)], row_s.at[o, away(k)])
        for k in range(1, H):
            wait_for(sel.at[o, :, mate(k)], row_s.at[o, mate(k)])
            if wide:
                wait_for(selx.at[o, :, mate(k) - base], rowx_s.at[o, mate(k) - base])
        for k in range(1, L):
            e = lax.rem(l + k, L)
            wait_for(outs.at[o, :, e], res_s.at[o, e])
        return carry

    lax.fori_loop(0, G, drain, 0)


def everywhere(tokens, routes, gate_weights, w_expert):
    T, D = tokens.shape
    picks = routes.shape[1]
    G = lax.axis_size("group")
    L = lax.axis_size("local")
    cap = T * picks // (G * L)
    FF = w_expert.shape[2]
    W, WF = tile_of(D, 256), tile_of(FF, 256)
    C, N, H = D // W, FF // WF, L // 2
    wide = C * WIDE // 14
    some = max(wide, 1)
    meta = jnp.concatenate(
        [routes.T.astype(jnp.float32), gate_weights.T.astype(jnp.float32)], axis=0
    )
    dma = pltpu.SemaphoreType.DMA
    bf16 = jnp.bfloat16
    return pl.pallas_call(
        functools.partial(fused_kernel, G, L, cap, W, WF, wide),
        out_shape=jax.ShapeDtypeStruct((T, FF), bf16),
        in_specs=[pl.BlockSpec(memory_space=pl.ANY)] * 3,
        out_specs=pl.BlockSpec(memory_space=pltpu.VMEM),
        scratch_shapes=[
            pltpu.VMEM((D, FF), bf16),
            pltpu.VMEM((G, C, T, W), bf16),
            pltpu.VMEM((G, some, T, W), bf16),
            pltpu.VMEM((G, 2 * picks, T), jnp.float32),
            pltpu.VMEM((G, 2 * picks, T), jnp.float32),
            pltpu.VMEM((G, L * cap, T), bf16),
            pltpu.VMEM((H * cap, T), bf16),
            pltpu.VMEM((G, L * cap, T), jnp.float32),
            pltpu.VMEM((G, C, L, cap, W), bf16),
            pltpu.VMEM((G, some, H, cap, W), bf16),
            pltpu.VMEM((G, C, L, cap, W), bf16),
            pltpu.VMEM((G, N, L, cap, WF), bf16),
            pltpu.VMEM((G, N, L, cap, WF), bf16),
            pltpu.VMEM((G, N, T, WF), bf16),
            pltpu.VMEM((G, N, T, WF), bf16),
            dma((2,)),
            dma((G,)),
            dma((G,)),
            dma((G,)),
            dma((G,)),
            dma,
            dma((G,)),
            dma((G,)),
            dma((G, C)),
            dma((G,)),
            dma((G,)),
            dma((G, some)),
            dma((G, L)),
            dma((G, H)),
            dma((G, L)),
            dma((G, L)),
            dma((G, N, L)),
            dma((G,)),
            dma((G, N)),
        ],
        compiler_params=pltpu.CompilerParams(
            collective_id=0, has_side_effects=True, vmem_limit_bytes=58 * 1024 * 1024
        ),
        cost_estimate=pl.CostEstimate(
            flops=2 * T * picks * D * FF, bytes_accessed=2 * D * FF, transcendentals=T * picks * FF
        ),
    )(tokens, meta, w_expert[0])


def solution(mesh):
    groups = mesh.shape["group"]

    def shards(tokens, routes, gate_weights, w_expert):
        if routes.shape[1] == 2 * groups:
            return everywhere(tokens, routes, gate_weights, w_expert)
        return routed(tokens, routes, gate_weights, w_expert)

    return jax.shard_map(
        shards,
        mesh=mesh,
        in_specs=(SPEC, SPEC, SPEC, P(("group", "local"), None, None)),
        out_specs=SPEC,
        check_vma=False,
    )
```
